32 devices in a mesh: parts: 2 (over y), group: 4 (over z), tile: 4 (over x, core).
Axes of the slice: x: 2, y: 2, z: 4, core: 2. Of those that a mesh axis runs over, the one named last changes fastest.
Arguments:
- product_codes: int32 [12288, 96], P(('parts', 'group', 'tile')), parts along dimension 0, may hold values from 0 to 255
- member_cluster: int32 [12288], P(('parts', 'group', 'tile')), parts along dimension 0, may hold values from 0 to 6143, as said below
- member_slot: int32 [12288], P(('parts', 'group', 'tile')), parts along dimension 0, may hold values from 0 to 12287, as said below
- codebook: bfloat16 [256, 768], replicated, may hold values from -14 to 14
Outputs:
- best_cosine: float32 [12288], P(('parts', 'group', 'tile')), parts along dimension 0
The draws below stay inside these ranges and needn't reach their ends.
There are 2 independent parts, one for each index of `parts`. The reference program is written for one: setup_inputs(seed, part) draws one part's arguments, and reference() takes and returns one part's arrays. A program takes and returns all parts, laid end to end along the dimension named above; an argument that names none is the same for every part. Nothing has to cross between parts.
Inputs may be any that keep to these rules, and one draw needn't show every extreme that they name: `member_slot`: distinct over the 6144 rows. Slot s belongs to the block of device s // 768 in group+tile order; all rows of one cluster have slots in one group's 4 * 768 consecutive slots. Of the 384 rows of one device at most 48 have slots in one device's block, and in every draw the last device's block receives exactly 48 rows from every device. `member_cluster`: rows with equal values form a cluster.
All inputs are finite; a program needn't handle non-finite values.
Results may differ from the reference program's by a relative error of at most 0.00054.
Values may be sent and summed in bfloat16 or wider, within the bound.
No kernel may reach another device: no remote copies, remote signals or barrier semaphores. Data moves between devices by JAX's collectives and lax.ppermute only.
A program may use at most 64 MiB of HBM per device.

```python
import jax
import jax.numpy as jnp
from jax import lax

SUBS = 96
CODES = 256
SUBDIM = 8
ROWS_DEV = 384
BLOCK = 768
ROWS = 6144
SLOTS = 12288
CLUSTER = 768
N_GROUP = 4
N_TILE = 4


def layout(key):
    device_count = ROWS // ROWS_DEV
    mean_load = ROWS_DEV // device_count
    middle_count = device_count - 2
    pair_count = middle_count // 2
    subkeys = jax.random.split(key, 5)
    shuffled = jax.random.permutation(subkeys[0], device_count).astype(jnp.int32)
    rotated = jnp.mod(shuffled - shuffled[0] - 1, device_count).astype(jnp.int32)
    bump = (rotated[1] == 0).astype(jnp.int32)
    ordering = jnp.where(rotated == device_count - 1, device_count - 1, jnp.mod(rotated + bump, device_count - 1)).astype(jnp.int32)
    spread = jax.random.randint(subkeys[1], (pair_count,), 0, mean_load)
    middle = jnp.stack([mean_load + spread, mean_load - spread], axis=1).reshape(middle_count).astype(jnp.int32)
    sorted_load = jnp.concatenate([jnp.array([2 * mean_load, 0], jnp.int32), middle])
    target_load = jnp.zeros((device_count,), jnp.int32).at[ordering].set(sorted_load)
    middle_rank = jnp.zeros((device_count,), jnp.int32).at[ordering].set(jnp.arange(device_count, dtype=jnp.int32) - 2)
    coins = jax.random.randint(subkeys[2], (middle_count,), 0, 2)
    swing = (coins - jnp.roll(coins, 1)).astype(jnp.int32)
    sources = jnp.arange(device_count, dtype=jnp.int32)
    lookup_index = jnp.mod(middle_rank[None, :] - sources[:, None], middle_count)
    count = target_load[None, :] + jnp.where(middle_rank[None, :] >= 0, swing[lookup_index], 0)
    cumulative = jnp.cumsum(count, axis=1)
    entries = jnp.arange(ROWS_DEV, dtype=jnp.int32)
    dest_of = jnp.sum((cumulative[:, None, :] <= entries[None, :, None]).astype(jnp.int32), axis=2)
    within = entries[None, :] - jnp.take_along_axis(cumulative - count, dest_of, axis=1)
    column_start = jnp.cumsum(count, axis=0) - count
    local = jnp.take_along_axis(column_start, dest_of, axis=1) + within
    filled = jnp.sum(count, axis=0)
    before = jnp.cumsum(filled) - filled
    fill_index = before[dest_of] + local
    flags = (jax.random.randint(subkeys[3], (ROWS,), 0, CLUSTER) == 0).astype(jnp.int32)
    flags = flags.at[before[::N_TILE]].set(1)
    cluster_of_fill = jnp.cumsum(flags) - 1
    last_cluster = cluster_of_fill[ROWS - 1]
    cluster_of_fill = jnp.where(cluster_of_fill == last_cluster, ROWS - 1, cluster_of_fill).astype(jnp.int32)
    row_cluster = cluster_of_fill[fill_index]
    shuffle = jax.vmap(lambda subkey: jax.random.permutation(subkey, ROWS_DEV))(jax.random.split(subkeys[4], device_count)).astype(jnp.int32)
    global_slot = dest_of * BLOCK + local
    slot_out = jnp.zeros((device_count, ROWS_DEV), jnp.int32).at[sources[:, None], shuffle].set(global_slot)
    cluster_out = jnp.zeros((device_count, ROWS_DEV), jnp.int32).at[sources[:, None], shuffle].set(row_cluster)
    return (slot_out.reshape(ROWS).astype(jnp.int32), cluster_out.reshape(ROWS).astype(jnp.int32))


def draw_member_slot(key, part):
    slot_out, cluster_out = layout(key)
    return slot_out


def draw_member_cluster(key, part):
    slot_out, cluster_out = layout(key)
    return cluster_out


def draw_product_codes(key, part):
    slot_out, cluster_out = layout(key)
    key = jax.random.fold_in(key, 3)
    subkeys = jax.random.split(key, 4)
    base_table = jax.random.randint(subkeys[0], (4096, SUBS), 0, CODES)
    base_codes = base_table[jnp.mod(cluster_out, 4096)]
    keep_share = jax.random.randint(subkeys[1], (ROWS, 1), 20, 97)
    keeping = jax.random.randint(subkeys[2], (ROWS, SUBS), 0, 100) < keep_share
    noise_codes = jax.random.randint(subkeys[3], (ROWS, SUBS), 0, CODES)
    return jnp.where(keeping, base_codes, noise_codes).astype(jnp.int32)


def draw_codebook(key, part):
    key = jax.random.fold_in(key, 7)
    subkeys = jax.random.split(key, 2)
    values = jnp.clip(jax.random.normal(subkeys[0], (CODES, SUBS, SUBDIM), jnp.float32), -4.5, 4.5)
    scales = jnp.exp(jax.random.uniform(subkeys[1], (CODES, SUBS, 1), jnp.float32, jnp.log(0.3), jnp.log(3.0)))
    return (values * scales).reshape(CODES, SUBS * SUBDIM).astype(jnp.bfloat16)


def setup_inputs(seed: int = 0, part: int = 0) -> dict:
    arg_keys = jax.random.split(jax.random.key(seed), 5)
    own_keys = jax.random.split(jax.random.fold_in(arg_keys[4], part), 5)
    product_codes = draw_product_codes(jax.random.fold_in(jax.random.fold_in(arg_keys[4], part), 71), part)
    member_cluster = draw_member_cluster(jax.random.fold_in(jax.random.fold_in(arg_keys[4], part), 71), part)
    member_slot = draw_member_slot(jax.random.fold_in(jax.random.fold_in(arg_keys[4], part), 71), part)
    codebook = draw_codebook(jax.random.fold_in(arg_keys[4], 71), part)
    return {"product_codes": product_codes, "member_cluster": member_cluster, "member_slot": member_slot, "codebook": codebook}


def reference(product_codes, member_cluster, member_slot, codebook):
    row_total = product_codes.shape[0]
    centroid_table = codebook.astype(jnp.float32).reshape(CODES, SUBS, SUBDIM)
    subspace = jnp.arange(SUBS, dtype=jnp.int32)[None, :]
    decoded = centroid_table[product_codes, subspace].reshape(row_total, SUBS * SUBDIM)
    inverse = lax.rsqrt(lax.optimization_barrier(jnp.sum(decoded * decoded, axis=1, keepdims=True)) + 1e-06)
    unit_rows = (decoded * inverse).astype(jnp.bfloat16)
    slot_rows = jnp.zeros((SLOTS, SUBS * SUBDIM), jnp.bfloat16).at[member_slot].set(unit_rows)
    slot_ids = jnp.full((SLOTS,), -1, jnp.int32).at[member_slot].set(member_cluster)
    group_slots = SLOTS // N_GROUP
    step_rows = 256

    def per_group(operands):
        group_rows, group_ids = operands
        column_index = jnp.arange(group_slots, dtype=jnp.int32)

        def per_block(first_row):
            block_rows = lax.dynamic_slice_in_dim(group_rows, first_row, step_rows, 0)
            block_ids = lax.dynamic_slice_in_dim(group_ids, first_row, step_rows, 0)
            row_index = first_row + jnp.arange(step_rows, dtype=jnp.int32)
            scores = lax.dot_general(block_rows, group_rows, (((1,), (1,)), ((), ())), preferred_element_type=jnp.float32)
            allowed = (block_ids[:, None] == group_ids[None, :]) & (block_ids[:, None] >= 0) & (column_index[None, :] < row_index[:, None])
            return lax.optimization_barrier(jnp.max(jnp.where(allowed, scores, -1.0), axis=1))
        starts = jnp.arange(0, group_slots, step_rows, dtype=jnp.int32)
        return lax.map(per_block, starts).reshape(group_slots)
    slot_best = lax.map(per_group, (slot_rows.reshape(N_GROUP, group_slots, SUBS * SUBDIM), slot_ids.reshape(N_GROUP, group_slots)))
    return slot_best.reshape(SLOTS)[member_slot]
```

```python
import functools

import jax
import jax.numpy as jnp
from jax import lax
from jax.experimental import pallas as pl
from jax.experimental.pallas import tpu as pltpu
from jax.sharding import PartitionSpec as P

LANES = 128
META_ROWS = 16
STEP = 256
AXES = ("group", "tile")


def gather_lanes(table, index):
    return jnp.take_along_axis(table, index, axis=1, mode="promise_in_bounds")


def lookup(low, high, codes):
    index = codes & (LANES - 1)
    return jnp.where(codes < LANES, gather_lanes(low, index), gather_lanes(high, index))


def unpack(packed, codes_ref):
    blocks, _, rows = codes_ref.shape
    subs = blocks * 8
    codes_ref[...] = packed[:subs].astype(jnp.float32).astype(jnp.int32).reshape(blocks, 8, rows)
    meta = packed[subs:].astype(jnp.float32).astype(jnp.int32)
    key = ((meta[3:4] * 256 + meta[2:3]) * 256 + meta[1:2]) * 256 + meta[0:1]
    return key, key - (meta[5:6] * 256 + meta[4:5])


def inverse_norms(codes_ref, norms_ref, chunk):
    total = jnp.zeros((8, LANES), jnp.float32)
    for block in range(codes_ref.shape[0]):
        rows = slice(block * 8, block * 8 + 8)
        codes = codes_ref[block, :, chunk * LANES : (chunk + 1) * LANES]
        total += lookup(norms_ref[rows, :LANES], norms_ref[rows, LANES:], codes)
    return lax.rsqrt(jnp.sum(total, axis=0, keepdims=True) + 1e-06)


def decode(codes_ref, table_ref, norms_ref, out_ref, column0):
    blocks, _, rows = codes_ref.shape
    sub_dim = table_ref.shape[0] // (blocks * 8)
    chunks = rows // LANES
    inverse = [jnp.broadcast_to(inverse_norms(codes_ref, norms_ref, c), (sub_dim, LANES)) for c in range(chunks)]

    def block(b, carry):
        for pair in range(4):
            first = pl.multiple_of(b * 8 * sub_dim + pair * 2 * sub_dim, 2 * sub_dim)
            pieces = [[] for _ in range(chunks)]
            for half in range(2):
                table = table_ref[pl.ds(first + half * sub_dim, sub_dim), :]
                sub = pair * 2 + half
                for c in range(chunks):
                    codes = codes_ref[b, sub : sub + 1, c * LANES : (c + 1) * LANES]
                    codes = jnp.broadcast_to(codes, (sub_dim, LANES))
                    pieces[c].append(lookup(table[:, :LANES], table[:, LANES:], codes) * inverse[c])
            for c in range(chunks):
                lanes = slice(column0 + c * LANES, column0 + (c + 1) * LANES)
                out_ref[pl.ds(first, 2 * sub_dim), lanes] = jnp.concatenate(pieces[c], axis=0).astype(jnp.bfloat16)
        return carry

    lax.fori_loop(0, blocks, block, 0)


def table_kernel(codebook_ref, own_ref, table_ref, norms_ref, rows_ref, codes_ref):
    subs = norms_ref.shape[0]
    table = codebook_ref[...].astype(jnp.float32).T
    table_ref[...] = table
    norms_ref[...] = jnp.sum((table * table).reshape(subs, table.shape[0] // subs, table.shape[1]), axis=1)
    unpack(own_ref[...], codes_ref)
    decode(codes_ref, table_ref, norms_ref, rows_ref, 0)


def columns_kernel(first_core, *refs):
    refs = list(refs)
    own_ref = refs.pop(0) if first_core else None
    count = len(refs) - 6
    inputs = refs[:count]
    table_ref, norms_ref, out_ref, key_ref, codes_ref, wide_ref = refs[count:]
    rows = codes_ref.shape[2]
    for k in range(count):
        packed = inputs[k][...]
        if k == 0 and first_core:
            core = lax.rem(lax.axis_index("tile"), 2)
            packed = jnp.where(core == 0, own_ref[...], packed)
        key, _ = unpack(packed, codes_ref)
        decode(codes_ref, table_ref, norms_ref, wide_ref, 0)
        for c in range(rows // LANES):
            lanes = slice(c * LANES, (c + 1) * LANES)
            target = slice(k * rows + c * LANES, k * rows + (c + 1) * LANES)
            out_ref[target, :] = wide_ref[:, lanes].T
            key_ref[target, :] = jnp.broadcast_to(key[:, lanes], (LANES, LANES)).T


def score(rows_ref, key, base, columns_ref, column_key_ref, best_ref):
    count = rows_ref.shape[1]

    def step(j, best):
        first = pl.multiple_of(j * STEP, STEP)
        columns = columns_ref[pl.ds(first, STEP), :]
        column_key = column_key_ref[pl.ds(first, STEP), :]
        out = []
        for n in range(count // STEP):
            lanes = slice(n * STEP, (n + 1) * STEP)
            scores = jnp.dot(columns, rows_ref[:, lanes], preferred_element_type=jnp.float32)
            keys = jnp.concatenate([column_key] * (STEP // LANES), axis=1)
            allowed = (keys < key[:, lanes]) & (keys >= base[:, lanes])
            scores = jnp.where(allowed, scores, -1.0)
            out.append(jnp.maximum(best[n], jnp.max(scores.reshape(STEP // 8, 8, STEP), axis=0)))
        return tuple(out)

    start = tuple(jnp.full((8, STEP), -1.0, jnp.float32) for _ in range(count // STEP))
    best = lax.fori_loop(0, columns_ref.shape[0] // STEP, step, start)
    for n in range(count // STEP):
        best_ref[:, n * STEP : (n + 1) * STEP] = jnp.max(best[n], axis=0, keepdims=True)


def far_kernel(direct_ref, passed_ref, table_ref, norms_ref, columns_ref, column_key_ref, best_ref, codes_ref, rows_ref):
    core = lax.rem(lax.axis_index("tile"), 2)
    key, base = unpack(jnp.where(core == 0, direct_ref[...], passed_ref[...]), codes_ref)
    decode(codes_ref, table_ref, norms_ref, rows_ref, 0)
    score(rows_ref, key, base, columns_ref, column_key_ref, best_ref)


def near_kernel(own_ref, rows_ref, columns_ref, column_key_ref, best_ref):
    subs = own_ref.shape[0] - META_ROWS
    meta = own_ref[subs:, :].astype(jnp.float32).astype(jnp.int32)
    key = ((meta[3:4] * 256 + meta[2:3]) * 256 + meta[1:2]) * 256 + meta[0:1]
    base = key - (meta[5:6] * 256 + meta[4:5])
    score(rows_ref, key, base, columns_ref, column_key_ref, best_ref)


PARAMS = pltpu.CompilerParams(vmem_limit_bytes=48 * 1024 * 1024)


def body(product_codes, member_cluster, member_slot, codebook):
    row_count, subs = product_codes.shape
    code_count, features = codebook.shape
    groups = lax.axis_size("group")
    tiles = lax.axis_size("tile")
    devices = groups * tiles
    pair_rows = 2 * row_count
    group_slots = tiles * 2 * row_count
    core = lax.axis_index("tile") % 2

    def exchange(value, offset_core0, offset_core1):
        pairs = [(i, i ^ (offset_core0 if i % 2 == 0 else offset_core1)) for i in range(devices)]
        return lax.ppermute(value, AXES, pairs)

    far = (groups // 2) * tiles
    chips = [dz * tiles + dx * 2 for dz in range(groups // 2) for dx in range(tiles // 2)]
    half = len(chips) // 2
    first_chips, second_chips = chips[:half], chips[half:][::-1]

    local = member_slot % group_slots
    key = member_cluster * group_slots + local
    digits = [key & 255, (key >> 8) & 255, (key >> 16) & 255, key >> 24, local & 255, local >> 8]
    meta = jnp.stack(digits + [jnp.zeros_like(key)] * (META_ROWS - len(digits)))
    packed = jnp.concatenate([product_codes.T, meta]).astype(jnp.bfloat16)
    sibling = exchange(packed, 1, 1)
    own = jnp.concatenate(
        [jnp.where(core == 0, packed, sibling), jnp.where(core == 0, sibling, packed)], axis=1
    )
    arrived = [
        exchange(own, far if k == 0 else first_chips[k], second_chips[k]) for k in range(half)
    ]

    shape = jax.ShapeDtypeStruct
    codes_scratch = pltpu.VMEM((subs // 8, 8, pair_rows), jnp.int32)
    wide_scratch = pltpu.VMEM((features, pair_rows), jnp.bfloat16)
    table, norms, own_rows = pl.pallas_call(
        table_kernel,
        out_shape=(
            shape((features, code_count), jnp.float32),
            shape((subs, code_count), jnp.float32),
            shape((features, pair_rows), jnp.bfloat16),
        ),
        scratch_shapes=[codes_scratch],
        compiler_params=PARAMS,
        name="decode_own",
    )(codebook, own)
    passed = exchange(arrived[0], 1, 1)

    far_best, near_best = None, None
    for k in range(0, half, 2):
        batch = arrived[k : k + 2]
        columns, column_key = pl.pallas_call(
            functools.partial(columns_kernel, k == 0),
            out_shape=(
                shape((len(batch) * pair_rows, features), jnp.bfloat16),
                shape((len(batch) * pair_rows, LANES), jnp.int32),
            ),
            scratch_shapes=[codes_scratch, wide_scratch],
            compiler_params=PARAMS,
            name="decode_columns",
        )(*([own] if k == 0 else []), *batch, table, norms)
        far_part = pl.pallas_call(
            far_kernel,
            out_shape=shape((1, pair_rows), jnp.float32),
            scratch_shapes=[codes_scratch, wide_scratch],
            compiler_params=PARAMS,
            name="score_far",
        )(arrived[0], passed, table, norms, columns, column_key)
        near_part = pl.pallas_call(
            near_kernel,
            out_shape=shape((1, pair_rows), jnp.float32),
            compiler_params=PARAMS,
            name="score_near",
        )(own, own_rows, columns, column_key)
        far_best = far_part if far_best is None else jnp.maximum(far_best, far_part)
        near_best = near_part if near_best is None else jnp.maximum(near_best, near_part)

    total = jnp.maximum(near_best, exchange(far_best, far, far))
    first, second = total[:, :row_count], total[:, row_count:]
    keep = jnp.where(core == 0, first, second)
    other = exchange(jnp.where(core == 0, second, first), 1, 1)
    return jnp.maximum(keep, other).reshape(row_count)


def solution(mesh):
    placed = (
        P(("parts", "group", "tile"), None),
        P(("parts", "group", "tile")),
        P(("parts", "group", "tile")),
        P(),
    )
    return jax.shard_map(
        body, mesh=mesh, in_specs=placed, out_specs=P(("parts", "group", "tile")), check_vma=False
    )
```

```python
import functools

import jax
import jax.numpy as jnp
from jax import lax
from jax.experimental import pallas as pl
from jax.experimental.pallas import tpu as pltpu
from jax.sharding import PartitionSpec as P

LANES = 128
META_ROWS = 16
BLOCK_SUBS = 16
STEP_ROWS = 768
STEP_LANES = 256
AXES = ("group", "tile")
GATHER = lax.GatherDimensionNumbers(
    offset_dims=(),
    collapsed_slice_dims=(1,),
    start_index_map=(1,),
    operand_batching_dims=(0,),
    start_indices_batching_dims=(0,),
)


def core_index():
    return lax.rem(lax.axis_index("tile"), 2)


def gather_lanes(table, index):
    return lax.gather(
        table, index[..., None], GATHER, slice_sizes=(1, 1), mode=lax.GatherScatterMode.PROMISE_IN_BOUNDS
    )


def integers(values):
    return values.astype(jnp.float32).astype(jnp.int32)


def read_keys(meta):
    meta = integers(meta)
    key = ((meta[3:4] * 256 + meta[2:3]) * 256 + meta[1:2]) * 256 + meta[0:1]
    return key, key - (meta[5:6] * 256 + meta[4:5])


def spread_keys(key, out_ref):
    for c in range(key.shape[1] // LANES):
        lanes = slice(c * LANES, (c + 1) * LANES)
        out_ref[lanes, :] = jnp.broadcast_to(key[:, lanes], (LANES, LANES)).T


def make_table(codebook_ref, table_ref, wide_ref, sub_dim):
    features = table_ref.shape[0]
    wide = codebook_ref[...].astype(jnp.float32).T
    for half in range(wide.shape[1] // LANES):
        lanes = slice(half * LANES, (half + 1) * LANES)
        wide_ref[...] = wide[:, lanes]
        for first in range(0, features, BLOCK_SUBS * sub_dim):
            for e in range(sub_dim):
                row = first + e * BLOCK_SUBS
                strided = wide_ref[pl.ds(first + e, BLOCK_SUBS, stride=sub_dim), :]
                table_ref[row : row + BLOCK_SUBS, lanes] = strided.astype(jnp.bfloat16)


def decode(codes, table_ref, exact_ref, out_ref):
    features = table_ref.shape[0]
    subs, rows = codes.shape
    sub_dim = features // subs
    for c in range(rows // LANES):
        lanes = slice(c * LANES, (c + 1) * LANES)
        total = jnp.zeros((8, LANES), jnp.float32)
        for block in range(subs // BLOCK_SUBS):
            chosen = integers(codes[block * BLOCK_SUBS : (block + 1) * BLOCK_SUBS, lanes]).astype(jnp.int16)
            index = chosen & (LANES - 1)
            in_low = chosen < LANES
            for e in range(sub_dim):
                row = (block * sub_dim + e) * BLOCK_SUBS
                table = table_ref[row : row + BLOCK_SUBS, :]
                low, high = gather_lanes(table[:, :LANES], index), gather_lanes(table[:, LANES:], index)
                exact = jnp.where(in_low, low, high)
                exact_ref[row : row + BLOCK_SUBS, lanes] = exact
                square = exact.astype(jnp.float32)
                square = square * square
                total = total + square[:8] + square[8:]
        inverse = lax.rsqrt(jnp.sum(total, axis=0, keepdims=True) + 1e-06)
        inverse = jnp.broadcast_to(inverse, (BLOCK_SUBS, LANES))
        for row in range(0, features, BLOCK_SUBS):
            exact = exact_ref[row : row + BLOCK_SUBS, lanes].astype(jnp.float32)
            out_ref[row : row + BLOCK_SUBS, lanes] = (exact * inverse).astype(jnp.bfloat16)


def meta_rows(cluster, slot, group_slots, groups):
    local = slot
    for g in range(1, groups):
        local = local - jnp.where(slot >= g * group_slots, group_slots, 0)
    key = cluster * group_slots + local
    digits = [key & 255, (key >> 8) & 255, (key >> 16) & 255, key >> 24, local & 255, local >> 8]
    row = lax.broadcasted_iota(jnp.int32, (META_ROWS, key.shape[1]), 0)
    meta = jnp.zeros(row.shape, jnp.int32)
    for d, digit in enumerate(digits):
        meta = jnp.where(row == d, digit, meta)
    return meta.astype(jnp.float32).astype(jnp.bfloat16)


def pack_kernel(group_slots, groups, codes_ref, cluster_ref, slot_ref, out_ref):
    subs, rows = codes_ref.shape
    out_ref[:subs, :] = codes_ref[...].astype(jnp.float32).astype(jnp.bfloat16)
    cluster, slot = cluster_ref[...].reshape(1, rows), slot_ref[...].reshape(1, rows)
    out_ref[subs:, :] = meta_rows(cluster, slot, group_slots, groups)


def join_kernel(group_slots, groups, packed_ref, codes_ref, cluster_ref, slot_ref, out_ref, other_ref):
    rows = packed_ref.shape[1]
    pack_kernel(group_slots, groups, codes_ref, cluster_ref, slot_ref, other_ref)
    first = core_index() == 0
    out_ref[:, :rows] = jnp.where(first, packed_ref[...], other_ref[...])
    out_ref[:, rows:] = jnp.where(first, other_ref[...], packed_ref[...])


def own_kernel(codebook_ref, packed_ref, table_ref, rows_ref, wide_ref, exact_ref):
    subs = packed_ref.shape[0] - META_ROWS
    make_table(codebook_ref, table_ref, wide_ref, codebook_ref.shape[1] // subs)
    decode(packed_ref[:subs, :], table_ref, exact_ref, rows_ref)


def columns_kernel(with_own, *refs):
    refs = list(refs)
    own_ref, own_rows_ref = (refs.pop(0), refs.pop(0)) if with_own else (None, None)
    packed_ref, table_ref, out_ref, key_ref, exact_ref, rows_ref = refs
    subs = packed_ref.shape[0] - META_ROWS
    decode(packed_ref[:subs, :], table_ref, exact_ref, rows_ref)
    if with_own:
        first = core_index() == 0
        out_ref[...] = jnp.where(first, own_rows_ref[...], rows_ref[...]).T
        key, _ = read_keys(jnp.where(first, own_ref[subs:, :], packed_ref[subs:, :]))
    else:
        out_ref[...] = rows_ref[...].T
        key, _ = read_keys(packed_ref[subs:, :])
    spread_keys(key, key_ref)


def score(rows_ref, meta, pairs, best_ref, so_far_ref=None):
    key, base = read_keys(meta)
    for n in range(rows_ref.shape[1] // STEP_LANES):
        lanes = slice(n * STEP_LANES, (n + 1) * STEP_LANES)
        best = jnp.full((8, STEP_LANES), -1.0, jnp.float32)
        for columns_ref, column_key_ref in pairs:
            for first in range(0, columns_ref.shape[0], STEP_ROWS):
                span = slice(first, first + STEP_ROWS)
                scores = jnp.dot(columns_ref[span, :], rows_ref[:, lanes], preferred_element_type=jnp.float32)
                keys = jnp.concatenate([column_key_ref[span, :]] * (STEP_LANES // LANES), axis=1)
                allowed = (keys < key[:, lanes]) & (keys >= base[:, lanes])
                scores = jnp.where(allowed, scores, -1.0)
                best = jnp.maximum(best, jnp.max(scores.reshape(STEP_ROWS // 8, 8, STEP_LANES), axis=0))
        best = jnp.max(best, axis=0, keepdims=True)
        best_ref[:, lanes] = best if so_far_ref is None else jnp.maximum(best, so_far_ref[:, lanes])


def far_first_kernel(
    direct_ref, passed_ref, table_ref, columns_ref, key_ref, meta_ref, rows_ref, best_ref, exact_ref
):
    subs = direct_ref.shape[0] - META_ROWS
    packed = jnp.where(core_index() == 0, direct_ref[...], passed_ref[...])
    meta_ref[...] = packed[subs:]
    decode(packed[:subs], table_ref, exact_ref, rows_ref)
    score(rows_ref, packed[subs:], [(columns_ref, key_ref)], best_ref)


def far_kernel(
    packed_ref, table_ref, meta_ref, far_rows_ref, so_far_ref, columns_ref, key_ref, best_ref, exact_ref, rows_ref
):
    columns_kernel(False, packed_ref, table_ref, columns_ref, key_ref, exact_ref, rows_ref)
    score(far_rows_ref, meta_ref[...], [(columns_ref, key_ref)], best_ref, so_far_ref)


def near_kernel(own_ref, rows_ref, *refs):
    *refs, best_ref = refs
    subs = own_ref.shape[0] - META_ROWS
    score(rows_ref, own_ref[subs:, :], list(zip(refs[::2], refs[1::2])), best_ref)


def call(kernel, microseconds, name, out_shape, scratch=()):
    return pl.pallas_call(
        kernel,
        out_shape=out_shape,
        scratch_shapes=scratch,
        compiler_params=pltpu.CompilerParams(vmem_limit_bytes=24 * 1024 * 1024),
        cost_estimate=pl.CostEstimate(flops=int(microseconds * 1.15e9), bytes_accessed=0, transcendentals=0),
        name=name,
    )


def body(product_codes, member_cluster, member_slot, codebook):
    row_count, subs = product_codes.shape
    code_count, features = codebook.shape
    groups = lax.axis_size("group")
    tiles = lax.axis_size("tile")
    devices = groups * tiles
    pair_rows = 2 * row_count
    group_slots = tiles * 2 * row_count
    packed_rows = subs + META_ROWS
    core = core_index()

    def exchange(value, offset_core0, offset_core1):
        pairs = [(i, i ^ (offset_core0 if i % 2 == 0 else offset_core1)) for i in range(devices)]
        return lax.ppermute(value, AXES, pairs)

    far = (groups // 2) * tiles
    chips = [dz * tiles + dx * 2 for dz in range(groups // 2) for dx in range(tiles // 2)]
    half = len(chips) // 2
    first_chips, second_chips = chips[:half], chips[half:]

    shape = jax.ShapeDtypeStruct
    bf16 = jnp.bfloat16
    exact_scratch = pltpu.VMEM((features, pair_rows), bf16)
    rows_shape = shape((features, pair_rows), bf16)
    columns_shape = shape((pair_rows, features), bf16)
    key_shape = shape((pair_rows, LANES), jnp.int32)
    best_shape = shape((1, pair_rows), jnp.float32)

    mine = (product_codes, member_cluster, member_slot)
    other_codes, other_cluster, other_slot = (exchange(value, 1, 1) for value in mine)
    packed = call(
        functools.partial(pack_kernel, group_slots, groups), 0.3, "pack", shape((packed_rows, row_count), bf16)
    )(product_codes.T, member_cluster, member_slot)
    own = call(
        functools.partial(join_kernel, group_slots, groups),
        0.3,
        "join",
        shape((packed_rows, pair_rows), bf16),
        [pltpu.VMEM((packed_rows, row_count), bf16)],
    )(packed, other_codes.T, other_cluster, other_slot)
    arrived = [exchange(own, far if k == 0 else first_chips[k], second_chips[k]) for k in range(half)]

    table, own_rows = call(
        own_kernel,
        1.2,
        "decode_own",
        (shape((features, code_count), bf16), rows_shape),
        [pltpu.VMEM((features, LANES), jnp.float32), exact_scratch],
    )(codebook, own)
    arrived[0], table = lax.optimization_barrier((arrived[0], table))
    passed = exchange(arrived[0], 1, 1)
    columns = call(
        functools.partial(columns_kernel, True),
        1.2,
        "columns_first",
        (columns_shape, key_shape),
        [exact_scratch, exact_scratch],
    )(own, own_rows, arrived[0], table)
    far_meta, far_rows, far_best = call(
        far_first_kernel,
        2.0,
        "far_first",
        (shape((META_ROWS, pair_rows), bf16), rows_shape, best_shape),
        [exact_scratch],
    )(arrived[0], passed, table, *columns)
    columns = [columns]
    for k in range(1, half):
        *latest, far_best = call(
            far_kernel, 2.0, "far_next", (columns_shape, key_shape, best_shape), [exact_scratch, exact_scratch]
        )(arrived[k], table, far_meta, far_rows, far_best)
        columns.append(latest)
    returned = exchange(far_best, far, far)
    near_best = None
    for k in range(0, half, 2):
        operands = [array for pair in columns[k : k + 2] for array in pair]
        part = call(near_kernel, 2.0, "near", best_shape)(own, own_rows, *operands)
        near_best = part if near_best is None else jnp.maximum(near_best, part)

    total = jnp.maximum(near_best, returned)
    first, second = total[:, :row_count], total[:, row_count:]
    keep = jnp.where(core == 0, first, second)
    other = exchange(jnp.where(core == 0, second, first), 1, 1)
    return jnp.maximum(keep, other).reshape(row_count)


def solution(mesh):
    placed = (
        P(("parts", "group", "tile"), None),
        P(("parts", "group", "tile")),
        P(("parts", "group", "tile")),
        P(),
    )
    return jax.shard_map(
        body, mesh=mesh, in_specs=placed, out_specs=P(("parts", "group", "tile")), check_vma=False
    )
```

```python
import functools

import jax
import jax.numpy as jnp
from jax import lax
from jax.experimental import pallas as pl
from jax.experimental.pallas import tpu as pltpu
from jax.sharding import PartitionSpec as P

LANES = 128
META_ROWS = 8
BLOCK_SUBS = 16
STEP_ROWS = 768
STEP_LANES = 256
AXES = ("group", "tile")
GATHER = lax.GatherDimensionNumbers(
    offset_dims=(),
    collapsed_slice_dims=(1,),
    start_index_map=(1,),
    operand_batching_dims=(0,),
    start_indices_batching_dims=(0,),
)


def core_index():
    return lax.rem(lax.axis_index("tile"), 2)


def gather_lanes(table, index):
    return lax.gather(
        table, index[..., None], GATHER, slice_sizes=(1, 1), mode=lax.GatherScatterMode.PROMISE_IN_BOUNDS
    )


def integers(values):
    return values.astype(jnp.float32).astype(jnp.int32)


def read_keys(meta):
    meta = integers(meta)
    key = ((meta[3:4] * 256 + meta[2:3]) * 256 + meta[1:2]) * 256 + meta[0:1]
    return key, key - (meta[5:6] * 256 + meta[4:5])


def spread_keys(key, out_ref):
    for c in range(key.shape[1] // LANES):
        lanes = slice(c * LANES, (c + 1) * LANES)
        out_ref[lanes, :] = jnp.broadcast_to(key[:, lanes], (LANES, LANES)).T


def make_table(codebook_ref, table_ref, wide_ref, sub_dim):
    features = table_ref.shape[0]
    wide = codebook_ref[...].astype(jnp.float32).T
    for half in range(wide.shape[1] // LANES):
        lanes = slice(half * LANES, (half + 1) * LANES)
        wide_ref[...] = wide[:, lanes]
        for first in range(0, features, BLOCK_SUBS * sub_dim):
            for e in range(sub_dim):
                row = first + e * BLOCK_SUBS
                strided = wide_ref[pl.ds(first + e, BLOCK_SUBS, stride=sub_dim), :]
                table_ref[row : row + BLOCK_SUBS, lanes] = strided.astype(jnp.bfloat16)


def decode(codes, table_ref, exact_ref, out_ref, chunks=None):
    features = table_ref.shape[0]
    subs, rows = codes.shape
    sub_dim = features // subs
    for c in range(rows // LANES) if chunks is None else chunks:
        lanes = slice(c * LANES, (c + 1) * LANES)
        total = jnp.zeros((8, LANES), jnp.float32)
        for block in range(subs // BLOCK_SUBS):
            chosen = integers(codes[block * BLOCK_SUBS : (block + 1) * BLOCK_SUBS, lanes]).astype(jnp.int16)
            index = chosen & (LANES - 1)
            in_low = chosen < LANES
            for e in range(sub_dim):
                row = (block * sub_dim + e) * BLOCK_SUBS
                table = table_ref[row : row + BLOCK_SUBS, :]
                low, high = gather_lanes(table[:, :LANES], index), gather_lanes(table[:, LANES:], index)
                exact = jnp.where(in_low, low, high)
                exact_ref[row : row + BLOCK_SUBS, lanes] = exact
                square = exact.astype(jnp.float32)
                square = square * square
                total = total + square[:8] + square[8:]
        inverse = lax.rsqrt(jnp.sum(total, axis=0, keepdims=True) + 1e-06)
        inverse = jnp.broadcast_to(inverse, (BLOCK_SUBS, LANES))
        for row in range(0, features, BLOCK_SUBS):
            exact = exact_ref[row : row + BLOCK_SUBS, lanes].astype(jnp.float32)
            out_ref[row : row + BLOCK_SUBS, lanes] = (exact * inverse).astype(jnp.bfloat16)


def meta_rows(cluster, slot, group_slots, groups):
    local = slot
    for g in range(1, groups):
        local = local - jnp.where(slot >= g * group_slots, group_slots, 0)
    key = cluster * group_slots + local
    digits = [key & 255, (key >> 8) & 255, (key >> 16) & 255, key >> 24, local & 255, local >> 8]
    row = lax.broadcasted_iota(jnp.int32, (META_ROWS, key.shape[1]), 0)
    meta = jnp.zeros(row.shape, jnp.int32)
    for d, digit in enumerate(digits):
        meta = jnp.where(row == d, digit, meta)
    return meta.astype(jnp.float32).astype(jnp.bfloat16)


def pack(codes, cluster, slot, group_slots, groups):
    subs, rows = codes.shape
    meta = meta_rows(cluster.reshape(1, rows), slot.reshape(1, rows), group_slots, groups)
    return codes.astype(jnp.float32).astype(jnp.bfloat16), meta


def pack_kernel(group_slots, groups, *refs):
    sources, out_ref, buffers, sems = refs[:3], refs[3], refs[4:7], refs[7]
    copies = [
        pltpu.make_async_copy(source, buffer, sems.at[k]) for k, (source, buffer) in enumerate(zip(sources, buffers))
    ]
    for copy in copies:
        copy.start()
    for copy in copies:
        copy.wait()
    codes, meta = pack(*(buffer[...] for buffer in buffers), group_slots, groups)
    out_ref[: codes.shape[0], :] = codes
    out_ref[codes.shape[0] :, :] = meta


def join_kernel(group_slots, groups, packed_ref, codes_ref, cluster_ref, slot_ref, out_ref):
    subs, rows = codes_ref.shape
    codes, meta = pack(codes_ref[...], cluster_ref[...], slot_ref[...], group_slots, groups)
    for half in range(2):
        mine = core_index() == half
        lanes = slice(half * rows, (half + 1) * rows)
        out_ref[:subs, lanes] = jnp.where(mine, packed_ref[:subs, :], codes)
        out_ref[subs:, lanes] = jnp.where(mine, packed_ref[subs:, :], meta)


def own_kernel(codebook_ref, packed_ref, table_ref, out_ref, wide_ref, exact_ref):
    subs = packed_ref.shape[0] - META_ROWS
    make_table(codebook_ref, table_ref, wide_ref, codebook_ref.shape[1] // subs)
    rows_kernel(packed_ref, table_ref, out_ref, exact_ref)


def rows_kernel(packed_ref, table_ref, out_ref, exact_ref):
    features = table_ref.shape[0]
    subs = packed_ref.shape[0] - META_ROWS
    decode(packed_ref[:subs, :], table_ref, exact_ref, out_ref)
    out_ref[features:, :] = packed_ref[subs:, :]


def columns_kernel(packed_ref, table_ref, columns_ref, key_ref, exact_ref, unit_ref):
    subs = packed_ref.shape[0] - META_ROWS
    decode(packed_ref[:subs, :], table_ref, exact_ref, unit_ref)
    columns_ref[...] = unit_ref[...].T
    spread_keys(read_keys(packed_ref[subs:, :])[0], key_ref)


def last_kernel(own_ref, packed_ref, table_ref, rows_ref, columns_ref, key_ref, exact_ref):
    features = columns_ref.shape[1]
    rows_kernel(packed_ref, table_ref, rows_ref, exact_ref)
    core0 = core_index() == 0
    columns_ref[...] = jnp.where(core0, own_ref[:features, :], rows_ref[:features, :]).T
    spread_keys(read_keys(jnp.where(core0, own_ref[features:, :], rows_ref[features:, :]))[0], key_ref)


def masked_max(columns_ref, key_ref, span, rows, key, base, best):
    scores = jnp.dot(columns_ref[span, :], rows, preferred_element_type=jnp.float32)
    keys = jnp.concatenate([key_ref[span, :]] * (scores.shape[1] // LANES), axis=1)
    scores = jnp.where((keys < key) & (keys >= base), scores, -1.0)
    return jnp.maximum(best, jnp.max(scores.reshape(scores.shape[0] // 8, 8, scores.shape[1]), axis=0))


def lane_steps(ref):
    return [slice(first, first + STEP_LANES) for first in range(0, ref.shape[1], STEP_LANES)]


def score(rows_ref, pairs, best_ref):
    features = pairs[0][0].shape[1]
    key, base = read_keys(rows_ref[features:, :])
    for lanes in lane_steps(rows_ref):
        best = jnp.full((8, STEP_LANES), -1.0, jnp.float32)
        for columns_ref, key_ref in pairs:
            for first in range(0, columns_ref.shape[0], STEP_ROWS):
                best = masked_max(
                    columns_ref,
                    key_ref,
                    slice(first, first + STEP_ROWS),
                    rows_ref[:features, lanes],
                    key[:, lanes],
                    base[:, lanes],
                    best,
                )
        best_ref[:, lanes] = jnp.max(best, axis=0, keepdims=True)


def far_kernel(direct_ref, passed_ref, table_ref, *refs):
    *columns, best_ref, rows_ref, exact_ref = refs
    core = core_index()

    @pl.when(core == 0)
    def _():
        rows_ref[...] = direct_ref[...]

    @pl.when(core != 0)
    def _():
        rows_kernel(passed_ref, table_ref, rows_ref, exact_ref)

    score(rows_ref, list(zip(columns[::2], columns[1::2])), best_ref)


def near_kernel(rows_ref, *refs):
    *columns, best_ref = refs
    score(rows_ref, list(zip(columns[::2], columns[1::2])), best_ref)


def call(kernel, microseconds, name, out_shape, scratch=(), in_specs=None):
    return pl.pallas_call(
        kernel,
        **({} if in_specs is None else {"in_specs": [in_specs] * 3}),
        out_shape=out_shape,
        scratch_shapes=scratch,
        compiler_params=pltpu.CompilerParams(vmem_limit_bytes=12 * 1024 * 1024),
        cost_estimate=pl.CostEstimate(flops=int(microseconds * 1.15e9), bytes_accessed=0, transcendentals=0),
        name=name,
    )


def body(product_codes, member_cluster, member_slot, codebook):
    row_count, subs = product_codes.shape
    code_count, features = codebook.shape
    groups = lax.axis_size("group")
    tiles = lax.axis_size("tile")
    devices = groups * tiles
    pair_rows = 2 * row_count
    group_slots = tiles * 2 * row_count
    packed_rows = subs + META_ROWS
    core = core_index()

    def exchange(value, offset_core0, offset_core1):
        pairs = [(i, i ^ (offset_core0 if i % 2 == 0 else offset_core1)) for i in range(devices)]
        return lax.ppermute(value, AXES, pairs)

    far = (groups // 2) * tiles
    chips = [dz * tiles + dx * 2 for dz in range(groups // 2) for dx in range(tiles // 2)]
    half = len(chips) // 2
    first_chips, second_chips = chips[:half], chips[half:]

    shape = jax.ShapeDtypeStruct
    bf16 = jnp.bfloat16
    exact_scratch = pltpu.VMEM((features, pair_rows), bf16)
    rows_shape = shape((features + META_ROWS, pair_rows), bf16)
    best_shape = shape((1, pair_rows), jnp.float32)

    mine = (product_codes, member_cluster, member_slot)
    other_codes, other_cluster, other_slot = (exchange(value, 1, 1) for value in mine)
    packed = call(
        functools.partial(pack_kernel, group_slots, groups),
        0.3,
        "pack",
        shape((packed_rows, row_count), bf16),
        [pltpu.VMEM((subs, row_count), jnp.int32)]
        + [pltpu.VMEM((row_count,), jnp.int32)] * 2
        + [pltpu.SemaphoreType.DMA((3,))],
        pl.BlockSpec(memory_space=pltpu.MemorySpace.HBM),
    )(*(pltpu.with_memory_space_constraint(v, pltpu.MemorySpace.HBM) for v in (product_codes.T, *mine[1:])))
    own = call(
        functools.partial(join_kernel, group_slots, groups),
        0.3,
        "join",
        shape((packed_rows, pair_rows), bf16),
    )(packed, other_codes.T, other_cluster, other_slot)
    arrived = [exchange(own, first_chips[k] or far, second_chips[k - 1]) for k in [*range(1, half), 0]]

    table, own_rows = call(
        own_kernel,
        1.2,
        "decode_own",
        (shape((features, code_count), bf16), rows_shape),
        [pltpu.VMEM((features, LANES), jnp.float32), exact_scratch],
    )(codebook, own)
    column_shapes = (shape((pair_rows, features), bf16), shape((pair_rows, LANES), jnp.int32))
    columns = []
    for latest in arrived[:-1]:
        latest, table, own_rows = lax.optimization_barrier((latest, table, own_rows))
        columns.append(
            call(columns_kernel, 1.2, "columns", column_shapes, [exact_scratch, exact_scratch])(latest, table)
        )
    last, table, columns = lax.optimization_barrier((arrived[-1], table, columns))
    passed = exchange(last, 1, 1)
    last_rows, *last_columns = call(last_kernel, 1.4, "last", (rows_shape, *column_shapes), [exact_scratch])(
        own_rows, last, table
    )
    columns.append(last_columns)
    rows_scratch = pltpu.VMEM(rows_shape.shape, bf16)
    far_best, near_best = None, None
    for k in range(0, half, 2):
        batch = [array for pair in columns[k : k + 2] for array in pair]
        far_part = call(far_kernel, 2.7, "score_far", best_shape, [rows_scratch, exact_scratch])(
            last_rows, passed, table, *batch
        )
        near_part = call(near_kernel, 2.0, "score_near", best_shape)(own_rows, *batch)
        far_best = far_part if far_best is None else jnp.maximum(far_best, far_part)
        near_best = near_part if near_best is None else jnp.maximum(near_best, near_part)

    returned = exchange(far_best, far, far)
    total = jnp.maximum(near_best, returned)
    first, second = total[:, :row_count], total[:, row_count:]
    keep = jnp.where(core == 0, first, second)
    other = exchange(jnp.where(core == 0, second, first), 1, 1)
    return jnp.maximum(keep, other).reshape(row_count)


def solution(mesh):
    placed = (
        P(("parts", "group", "tile"), None),
        P(("parts", "group", "tile")),
        P(("parts", "group", "tile")),
        P(),
    )
    return jax.shard_map(
        body, mesh=mesh, in_specs=placed, out_specs=P(("parts", "group", "tile")), check_vma=False
    )
```

```python
import functools

import jax
import jax.numpy as jnp
from jax import lax
from jax.experimental import pallas as pl
from jax.experimental.pallas import tpu as pltpu
from jax.sharding import PartitionSpec as P

LANES = 128
META_ROWS = 8
VMEM_LIMIT = 8 * 1024 * 1024
BLOCK_SUBS = 16
STEP_LANES = 256
AXES = ("group", "tile")
GATHER = lax.GatherDimensionNumbers(
    offset_dims=(),
    collapsed_slice_dims=(1,),
    start_index_map=(1,),
    operand_batching_dims=(0,),
    start_indices_batching_dims=(0,),
)


def gather_lanes(table, index):
    return lax.gather(
        table, index[..., None], GATHER, slice_sizes=(1, 1), mode=lax.GatherScatterMode.PROMISE_IN_BOUNDS
    )


def integers(values):
    return values.astype(jnp.float32).astype(jnp.int32)


def read_keys(meta):
    meta = integers(meta)
    key = ((meta[3:4] * 256 + meta[2:3]) * 256 + meta[1:2]) * 256 + meta[0:1]
    return key, key - (meta[5:6] * 256 + meta[4:5])


def spread_keys(key, out_ref):
    for c in range(key.shape[1] // LANES):
        lanes = slice(c * LANES, (c + 1) * LANES)
        out_ref[lanes, :] = jnp.broadcast_to(key[:, lanes], (LANES, LANES)).T


def make_table(codebook_ref, table_ref, wide_ref, sub_dim):
    features = table_ref.shape[0]
    wide = codebook_ref[...].astype(jnp.float32).T
    for half in range(wide.shape[1] // LANES):
        lanes = slice(half * LANES, (half + 1) * LANES)
        wide_ref[...] = wide[:, lanes]
        for first in range(0, features, BLOCK_SUBS * sub_dim):
            for e in range(sub_dim):
                row = first + e * BLOCK_SUBS
                strided = wide_ref[pl.ds(first + e, BLOCK_SUBS, stride=sub_dim), :]
                table_ref[row : row + BLOCK_SUBS, lanes] = strided.astype(jnp.bfloat16)


def decode(codes, table_ref, exact_ref, out_ref, chunks=None):
    features = table_ref.shape[0]
    subs, rows = codes.shape
    sub_dim = features // subs
    for c in range(rows // LANES) if chunks is None else chunks:
        lanes = slice(c * LANES, (c + 1) * LANES)
        total = jnp.zeros((8, LANES), jnp.float32)
        for block in range(subs // BLOCK_SUBS):
            chosen = integers(codes[block * BLOCK_SUBS : (block + 1) * BLOCK_SUBS, lanes]).astype(jnp.int16)
            index = chosen & (LANES - 1)
            in_low = chosen < LANES
            for e in range(sub_dim):
                row = (block * sub_dim + e) * BLOCK_SUBS
                table = table_ref[row : row + BLOCK_SUBS, :]
                low, high = gather_lanes(table[:, :LANES], index), gather_lanes(table[:, LANES:], index)
                exact = jnp.where(in_low, low, high)
                exact_ref[row : row + BLOCK_SUBS, lanes] = exact
                square = exact.astype(jnp.float32)
                square = square * square
                total = total + square[:8] + square[8:]
        inverse = lax.rsqrt(jnp.sum(total, axis=0, keepdims=True) + 1e-06)
        inverse = jnp.broadcast_to(inverse, (BLOCK_SUBS, LANES))
        for row in range(0, features, BLOCK_SUBS):
            exact = exact_ref[row : row + BLOCK_SUBS, lanes].astype(jnp.float32)
            out_ref[row : row + BLOCK_SUBS, lanes] = (exact * inverse).astype(jnp.bfloat16)


def meta_rows(cluster, slot, group_slots, groups):
    local = slot
    for g in range(1, groups):
        local = local - jnp.where(slot >= g * group_slots, group_slots, 0)
    key = cluster * group_slots + local
    digits = [key & 255, (key >> 8) & 255, (key >> 16) & 255, key >> 24, local & 255, local >> 8]
    row = lax.broadcasted_iota(jnp.int32, (META_ROWS, key.shape[1]), 0)
    meta = jnp.zeros(row.shape, jnp.int32)
    for d, digit in enumerate(digits):
        meta = jnp.where(row == d, digit, meta)
    return meta.astype(jnp.float32).astype(jnp.bfloat16)


def pack(codes, cluster, slot, group_slots, groups):
    subs, rows = codes.shape
    meta = meta_rows(cluster.reshape(1, rows), slot.reshape(1, rows), group_slots, groups)
    return codes.astype(jnp.float32).astype(jnp.bfloat16), meta


def pack_kernel(group_slots, groups, *refs):
    sources, out_ref, buffers, sems = refs[:3], refs[3], refs[4:7], refs[7]
    copies = [
        pltpu.make_async_copy(source, buffer, sems.at[k]) for k, (source, buffer) in enumerate(zip(sources, buffers))
    ]
    for copy in copies:
        copy.start()
    for copy in copies:
        copy.wait()
    codes, meta = pack(*(buffer[...] for buffer in buffers), group_slots, groups)
    out_ref[: codes.shape[0], :] = codes
    out_ref[codes.shape[0] :, :] = meta


def join_kernel(group_slots, groups, packed_ref, codes_ref, cluster_ref, slot_ref, out_ref):
    subs, rows = codes_ref.shape
    codes, meta = pack(codes_ref[...], cluster_ref[...], slot_ref[...], group_slots, groups)
    out_ref[:, :rows] = packed_ref[...]
    out_ref[:subs, rows:] = codes
    out_ref[subs:, rows:] = meta


def unit_kernel(packed_ref, table_ref, out_ref, exact_ref):
    features = table_ref.shape[0]
    subs = packed_ref.shape[0] - META_ROWS
    decode(packed_ref[:subs, :], table_ref, exact_ref, out_ref)
    out_ref[features:, :] = packed_ref[subs:, :]


def turn(unit_ref, rows_ref, key_ref, base_ref):
    rows, features = rows_ref.shape
    rows_ref[...] = unit_ref[:features, :rows].T
    key, base = read_keys(unit_ref[features:, :rows])
    spread_keys(key, key_ref)
    spread_keys(base, base_ref)


def score(rows_ref, key_ref, base_ref, unit_refs, best):
    features = rows_ref.shape[1]
    for unit_ref in unit_refs:
        count = unit_ref.shape[1]
        column_key, _ = read_keys(unit_ref[features:, :])
        for first in range(0, count, STEP_LANES):
            span = slice(first, min(first + STEP_LANES, count))
            scores = jnp.dot(rows_ref[...], unit_ref[:features, span], preferred_element_type=jnp.float32)
            for c in range(0, scores.shape[1], LANES):
                keys = column_key[:, first + c : first + c + LANES]
                allowed = (keys < key_ref[...]) & (keys >= base_ref[...])
                best = jnp.maximum(best, jnp.where(allowed, scores[:, c : c + LANES], -1.0))
    return best


def nothing(shape):
    return jnp.full(shape, -1.0, jnp.float32)


def finish(best):
    rows = best.shape[0]
    pieces = [
        jnp.max(best[first : first + LANES, :].T, axis=0, keepdims=True) for first in range(0, rows, LANES)
    ]
    return jnp.concatenate(pieces, axis=1)


def own_kernel(codebook_ref, packed_ref, table_ref, unit_ref, rows_ref, key_ref, base_ref, wide_ref, exact_ref):
    subs = packed_ref.shape[0] - META_ROWS
    make_table(codebook_ref, table_ref, wide_ref, table_ref.shape[0] // subs)
    unit_kernel(packed_ref, table_ref, unit_ref, exact_ref)
    turn(unit_ref, rows_ref, key_ref, base_ref)


def far_kernel(packed_ref, table_ref, rows_ref, key_ref, base_ref, unit_ref, exact_ref):
    unit_kernel(packed_ref, table_ref, unit_ref, exact_ref)
    turn(unit_ref, rows_ref, key_ref, base_ref)


def step_kernel(plan, whole, *refs):
    refs = list(refs)
    take = lambda count: [refs.pop(0) for _ in range(count)]
    jobs = [(take(3), take(ready), take(1) if so_far else None) for ready, so_far in plan]
    if len(refs) > len(plan):
        table_ref, packed_ref, out_ref = take(3)
        unit_kernel(packed_ref, table_ref, out_ref, refs[-1])
    for (rows, unit_refs, so_far), best_ref in zip(jobs, refs):
        best = so_far[0][...] if so_far else nothing((rows[0].shape[0], LANES))
        best = score(*rows, unit_refs, best)
        best_ref[...] = finish(best) if whole else best


VMEM = pl.BlockSpec(memory_space=pltpu.MemorySpace.VMEM)
HBM = pl.BlockSpec(memory_space=pltpu.MemorySpace.HBM)


def call(kernel, microseconds, name, out_shape, scratch=(), in_spec=VMEM):
    def run(*operands):
        return pl.pallas_call(
            kernel,
            in_specs=[in_spec] * len(operands),
            out_shape=out_shape,
            scratch_shapes=scratch,
            compiler_params=pltpu.CompilerParams(vmem_limit_bytes=VMEM_LIMIT),
            cost_estimate=pl.CostEstimate(flops=int(microseconds * 1.15e9), bytes_accessed=0, transcendentals=0),
            name=name,
        )(*operands)

    return run


def body(product_codes, member_cluster, member_slot, codebook):
    row_count, subs = product_codes.shape
    code_count, features = codebook.shape
    groups = lax.axis_size("group")
    tiles = lax.axis_size("tile")
    devices = groups * tiles
    pair_rows = 2 * row_count
    group_slots = tiles * 2 * row_count
    packed_rows = subs + META_ROWS

    def exchange(value, offset_core0, offset_core1):
        pairs = [(i, i ^ (offset_core0 if i % 2 == 0 else offset_core1)) for i in range(devices)]
        return lax.ppermute(value, AXES, pairs)

    far = (groups // 2) * tiles
    chips = [dz * tiles + dx * 2 for dz in range(groups // 2) for dx in range(tiles // 2)]
    pairs, last_chip = list(zip(chips[1:-1:2], chips[2:-1:2])), chips[-1]

    shape = jax.ShapeDtypeStruct
    bf16 = jnp.bfloat16

    def exact(count):
        return pltpu.VMEM((features, count), bf16)

    def unit(count):
        return shape((features + META_ROWS, count), bf16)

    spread = shape((row_count, LANES), jnp.int32)
    turned = (shape((row_count, features), bf16), spread, spread)
    lane_best = shape((row_count, LANES), jnp.float32)
    row_best = shape((1, row_count), jnp.float32)

    mine = (product_codes, member_cluster, member_slot)
    other_codes, other_cluster, other_slot = (exchange(value, 1, 1) for value in mine)
    packed = call(
        functools.partial(pack_kernel, group_slots, groups),
        0.3,
        "pack",
        shape((packed_rows, row_count), bf16),
        [pltpu.VMEM((subs, row_count), jnp.int32)]
        + [pltpu.VMEM((row_count,), jnp.int32)] * 2
        + [pltpu.SemaphoreType.DMA((3,))],
        in_spec=HBM,
    )(*(pltpu.with_memory_space_constraint(v, pltpu.MemorySpace.HBM) for v in (product_codes.T, *mine[1:])))
    own = call(
        functools.partial(join_kernel, group_slots, groups), 0.3, "join", shape((packed_rows, pair_rows), bf16)
    )(packed, other_codes.T, other_cluster, other_slot)
    packed, own = lax.optimization_barrier((packed, own))
    from_far = exchange(packed, far, far)
    arrived = [exchange(own, *pair) for pair in pairs]
    last = exchange(packed, last_chip, last_chip)

    table, own_unit, *own_rows = call(
        own_kernel,
        1.4,
        "decode_own",
        (shape((features, code_count), bf16), unit(pair_rows), *turned),
        [pltpu.VMEM((features, LANES), jnp.float32), exact(pair_rows)],
    )(codebook, own)

    def step(name, jobs, packed=None, whole=False):
        out_shape = [row_best if whole else lane_best for _ in jobs]
        operands, plan, decode_time, score_time = [], [], 0.0, 0.0
        for rows, ready, so_far in jobs:
            operands += [*rows, *ready, *([] if so_far is None else [so_far])]
            plan.append((len(ready), so_far is not None))
            score_time += sum(u.shape[1] for u in ready) * 0.0007
        scratch = []
        if packed is not None:
            out_shape.insert(0, unit(packed.shape[1]))
            operands += [table, packed]
            decode_time = packed.shape[1] * 0.0011
            scratch = [exact(packed.shape[1])]
        kernel = functools.partial(step_kernel, plan, whole)
        return call(kernel, 0.2 + max(decode_time, score_time), name, out_shape, scratch)(*operands)

    first, table, own_unit = lax.optimization_barrier((arrived[0], table, own_unit))
    passed = exchange(first, 1, 1)
    first_unit, near_best = step("first", [(own_rows, [own_unit], None)], first)
    from_far, near_best = lax.optimization_barrier((from_far, near_best))
    far_rows = call(
        far_kernel, 0.9, "far", turned, [pltpu.VMEM(unit(row_count).shape, bf16), exact(row_count)]
    )(from_far, table)
    last, far_rows = lax.optimization_barrier((last, far_rows))
    last_passed = exchange(last, 1, 1)
    waiting, far_best = step("second", [(far_rows, [own_unit, first_unit], None)], passed)
    units = [first_unit, waiting]
    for latest in [codes for received in arrived[1:] for codes in (received, exchange(received, 1, 1))] + [last, last_passed]:
        waiting, far_best = step("more", [(far_rows, [waiting], far_best)], latest)
        units.append(waiting)
    (far_best,) = step("far_rest", [(far_rows, [waiting], far_best)], whole=True)
    best = exchange(far_best, far, far)
    for k in range(0, len(units), 4):
        (part,) = step("near_rest", [(own_rows, units[k : k + 4], near_best)], whole=True)
        best = jnp.maximum(best, part)
    return best.reshape(row_count)


def solution(mesh):
    placed = (
        P(("parts", "group", "tile"), None),
        P(("parts", "group", "tile")),
        P(("parts", "group", "tile")),
        P(),
    )
    return jax.shard_map(
        body, mesh=mesh, in_specs=placed, out_specs=P(("parts", "group", "tile")), check_vma=False
    )
```

```python
import functools

import jax
import jax.numpy as jnp
from jax import lax
from jax.experimental import pallas as pl
from jax.experimental.pallas import tpu as pltpu
from jax.sharding import PartitionSpec as P

LANES = 128
META_ROWS = 8
VMEM_LIMIT = 8 * 1024 * 1024
BLOCK_SUBS = 16
STEP_LANES = 256
AXES = ("group", "tile")
GATHER = lax.GatherDimensionNumbers(
    offset_dims=(),
    collapsed_slice_dims=(1,),
    start_index_map=(1,),
    operand_batching_dims=(0,),
    start_indices_batching_dims=(0,),
)


def gather_lanes(table, index):
    return lax.gather(
        table, index[..., None], GATHER, slice_sizes=(1, 1), mode=lax.GatherScatterMode.PROMISE_IN_BOUNDS
    )


def integers(values):
    return values.astype(jnp.float32).astype(jnp.int32)


def read_keys(meta):
    meta = integers(meta)
    key = ((meta[3:4] * 256 + meta[2:3]) * 256 + meta[1:2]) * 256 + meta[0:1]
    return key, key - (meta[5:6] * 256 + meta[4:5])


def spread_keys(key, out_ref):
    for c in range(key.shape[1] // LANES):
        lanes = slice(c * LANES, (c + 1) * LANES)
        out_ref[lanes, :] = jnp.broadcast_to(key[:, lanes], (LANES, LANES)).T


def make_table(codebook_ref, table_ref, wide_ref, sub_dim):
    features = table_ref.shape[0]
    wide = codebook_ref[...].astype(jnp.float32).T
    for half in range(wide.shape[1] // LANES):
        lanes = slice(half * LANES, (half + 1) * LANES)
        wide_ref[...] = wide[:, lanes]
        for first in range(0, features, BLOCK_SUBS * sub_dim):
            for e in range(sub_dim):
                row = first + e * BLOCK_SUBS
                strided = wide_ref[pl.ds(first + e, BLOCK_SUBS, stride=sub_dim), :]
                table_ref[row : row + BLOCK_SUBS, lanes] = strided.astype(jnp.bfloat16)


def decode(codes, table_ref, exact_ref, out_ref, column0):
    features = table_ref.shape[0]
    subs, rows = codes.shape
    sub_dim = features // subs
    for c in range(rows // LANES):
        lanes = slice(c * LANES, (c + 1) * LANES)
        out_lanes = slice(column0 + c * LANES, column0 + (c + 1) * LANES)
        total = jnp.zeros((8, LANES), jnp.float32)
        for block in range(subs // BLOCK_SUBS):
            chosen = integers(codes[block * BLOCK_SUBS : (block + 1) * BLOCK_SUBS, lanes]).astype(jnp.int16)
            index = chosen & (LANES - 1)
            in_low = chosen < LANES
            for e in range(sub_dim):
                row = (block * sub_dim + e) * BLOCK_SUBS
                table = table_ref[row : row + BLOCK_SUBS, :]
                low, high = gather_lanes(table[:, :LANES], index), gather_lanes(table[:, LANES:], index)
                exact = jnp.where(in_low, low, high)
                exact_ref[row : row + BLOCK_SUBS, lanes] = exact
                square = exact.astype(jnp.float32)
                square = square * square
                total = total + square[:8] + square[8:]
        inverse = lax.rsqrt(jnp.sum(total, axis=0, keepdims=True) + 1e-06)
        inverse = jnp.broadcast_to(inverse, (BLOCK_SUBS, LANES))
        for row in range(0, features, BLOCK_SUBS):
            exact = exact_ref[row : row + BLOCK_SUBS, lanes].astype(jnp.float32)
            out_ref[row : row + BLOCK_SUBS, out_lanes] = (exact * inverse).astype(jnp.bfloat16)


def meta_rows(cluster, slot, group_slots, groups):
    local = slot
    for g in range(1, groups):
        local = local - jnp.where(slot >= g * group_slots, group_slots, 0)
    key = cluster * group_slots + local
    digits = [key & 255, (key >> 8) & 255, (key >> 16) & 255, key >> 24, local & 255, local >> 8]
    row = lax.broadcasted_iota(jnp.int32, (META_ROWS, key.shape[1]), 0)
    meta = jnp.zeros(row.shape, jnp.int32)
    for d, digit in enumerate(digits):
        meta = jnp.where(row == d, digit, meta)
    return meta.astype(jnp.float32).astype(jnp.bfloat16)


def pack(codes, cluster, slot, group_slots, groups):
    subs, rows = codes.shape
    meta = meta_rows(cluster.reshape(1, rows), slot.reshape(1, rows), group_slots, groups)
    return codes.astype(jnp.float32).astype(jnp.bfloat16), meta


def pack_kernel(group_slots, groups, *refs):
    sources, out_ref, buffers, sems = refs[:3], refs[3], refs[4:7], refs[7]
    copies = [
        pltpu.make_async_copy(source, buffer, sems.at[k]) for k, (source, buffer) in enumerate(zip(sources, buffers))
    ]
    for copy in copies:
        copy.start()
    for copy in copies:
        copy.wait()
    codes, meta = pack(*(buffer[...] for buffer in buffers), group_slots, groups)
    out_ref[: codes.shape[0], :] = codes
    out_ref[codes.shape[0] :, :] = meta


def join_kernel(group_slots, groups, packed_ref, codes_ref, cluster_ref, slot_ref, out_ref):
    subs, rows = codes_ref.shape
    codes, meta = pack(codes_ref[...], cluster_ref[...], slot_ref[...], group_slots, groups)
    out_ref[:, :rows] = packed_ref[...]
    out_ref[:subs, rows:] = codes
    out_ref[subs:, rows:] = meta


def unit_kernel(packed_ref, table_ref, out_ref, exact_ref, column0=0):
    features = table_ref.shape[0]
    subs, rows = packed_ref.shape[0] - META_ROWS, packed_ref.shape[1]
    decode(packed_ref[:subs, :], table_ref, exact_ref, out_ref, column0)
    out_ref[features:, column0 : column0 + rows] = packed_ref[subs:, :]


def turn(unit_ref, rows_ref, base_ref, slot_ref):
    rows, features = rows_ref.shape
    rows_ref[...] = unit_ref[:features, :rows].T
    key, base = read_keys(unit_ref[features:, :rows])
    spread_keys(base, base_ref)
    spread_keys(key - base, slot_ref)


def score(rows_ref, base_ref, slot_ref, unit_refs, best):
    features = rows_ref.shape[1]
    for unit_ref in unit_refs:
        count = unit_ref.shape[1]
        column_key, _ = read_keys(unit_ref[features:, :])
        for first in range(0, count, STEP_LANES):
            span = slice(first, min(first + STEP_LANES, count))
            scores = jnp.dot(rows_ref[...], unit_ref[:features, span], preferred_element_type=jnp.float32)
            for c in range(0, scores.shape[1], LANES):
                distance = column_key[:, first + c : first + c + LANES] - base_ref[...]
                allowed = distance.astype(jnp.uint32) < slot_ref[...].astype(jnp.uint32)
                best = jnp.maximum(best, jnp.where(allowed, scores[:, c : c + LANES], -1.0))
    return best


def nothing(shape):
    return jnp.full(shape, -1.0, jnp.float32)


def finish(best):
    rows = best.shape[0]
    pieces = [
        jnp.max(best[first : first + LANES, :].T, axis=0, keepdims=True) for first in range(0, rows, LANES)
    ]
    return jnp.concatenate(pieces, axis=1)


def own_kernel(codebook_ref, packed_ref, table_ref, unit_ref, wide_ref, exact_ref):
    subs = packed_ref.shape[0] - META_ROWS
    make_table(codebook_ref, table_ref, wide_ref, table_ref.shape[0] // subs)
    unit_kernel(packed_ref, table_ref, unit_ref, exact_ref)


def decode_kernel(*refs):
    packed_ref, table_ref, unit_ref, exact_ref = refs
    unit_kernel(packed_ref, table_ref, unit_ref, exact_ref)


def near_kernel(own_ref, *refs):
    *unit_refs, best_ref, rows_ref, key_ref, base_ref = refs
    turn(own_ref, rows_ref, key_ref, base_ref)
    best_ref[...] = finish(score(rows_ref, key_ref, base_ref, unit_refs, nothing(key_ref.shape)))


def far_kernel(packed_ref, table_ref, rows_ref, key_ref, base_ref, unit_ref, exact_ref):
    unit_kernel(packed_ref, table_ref, unit_ref, exact_ref)
    turn(unit_ref, rows_ref, key_ref, base_ref)


def step_kernel(ready, with_so_far, decoded, whole, *refs):
    refs = list(refs)
    take = lambda count: [refs.pop(0) for _ in range(count)]
    rows, unit_refs, so_far = take(3), take(ready), take(with_so_far)
    table_refs, packed_refs, out_refs = take(min(decoded, 1)), take(decoded), take(min(decoded, 1))
    best_ref, exact_refs = refs[0], refs[1:]
    column0 = 0
    for packed_ref, exact_ref in zip(packed_refs, exact_refs):
        unit_kernel(packed_ref, table_refs[0], out_refs[0], exact_ref, column0)
        column0 += packed_ref.shape[1]
    best = score(*rows, unit_refs, so_far[0][...] if so_far else nothing((rows[0].shape[0], LANES)))
    best_ref[...] = finish(best) if whole else best


VMEM = pl.BlockSpec(memory_space=pltpu.MemorySpace.VMEM)
HBM = pl.BlockSpec(memory_space=pltpu.MemorySpace.HBM)


def call(kernel, microseconds, name, out_shape, scratch=(), in_spec=VMEM):
    def run(*operands):
        return pl.pallas_call(
            kernel,
            in_specs=[in_spec] * len(operands),
            out_shape=out_shape,
            scratch_shapes=scratch,
            compiler_params=pltpu.CompilerParams(vmem_limit_bytes=VMEM_LIMIT),
            cost_estimate=pl.CostEstimate(flops=int(microseconds * 1.15e9), bytes_accessed=0, transcendentals=0),
            name=name,
        )(*operands)

    return run


def body(product_codes, member_cluster, member_slot, codebook):
    row_count, subs = product_codes.shape
    code_count, features = codebook.shape
    groups = lax.axis_size("group")
    tiles = lax.axis_size("tile")
    devices = groups * tiles
    pair_rows = 2 * row_count
    group_slots = tiles * 2 * row_count
    packed_rows = subs + META_ROWS

    def exchange(value, offset_core0, offset_core1):
        pairs = [(i, i ^ (offset_core0 if i % 2 == 0 else offset_core1)) for i in range(devices)]
        return lax.ppermute(value, AXES, pairs)

    far = (groups // 2) * tiles
    chips = [dz * tiles + dx * 2 for dz in range(groups // 2) for dx in range(tiles // 2)]
    pairs, last_chip = list(zip(chips[1:-1:2], chips[2:-1:2])), chips[-1]

    shape = jax.ShapeDtypeStruct
    bf16 = jnp.bfloat16

    def exact(count):
        return pltpu.VMEM((features, count), bf16)

    def unit(count):
        return shape((features + META_ROWS, count), bf16)

    spread = shape((row_count, LANES), jnp.int32)
    turned = (shape((row_count, features), bf16), spread, spread)
    lane_best = shape((row_count, LANES), jnp.float32)
    row_best = shape((1, row_count), jnp.float32)

    mine = (product_codes, member_cluster, member_slot)
    other_codes, other_cluster, other_slot = (exchange(value, 1, 1) for value in mine)
    packed = call(
        functools.partial(pack_kernel, group_slots, groups),
        0.3,
        "pack",
        shape((packed_rows, row_count), bf16),
        [pltpu.VMEM((subs, row_count), jnp.int32)]
        + [pltpu.VMEM((row_count,), jnp.int32)] * 2
        + [pltpu.SemaphoreType.DMA((3,))],
        in_spec=HBM,
    )(*(pltpu.with_memory_space_constraint(v, pltpu.MemorySpace.HBM) for v in (product_codes.T, *mine[1:])))
    own = call(
        functools.partial(join_kernel, group_slots, groups), 0.3, "join", shape((packed_rows, pair_rows), bf16)
    )(packed, other_codes.T, other_cluster, other_slot)
    packed, own = lax.optimization_barrier((packed, own))
    from_far = exchange(packed, far, far)
    arrived = [exchange(own, *pair) for pair in pairs]
    last = exchange(packed, last_chip, last_chip)

    table, own_unit = call(
        own_kernel,
        1.4,
        "decode_own",
        (shape((features, code_count), bf16), unit(pair_rows)),
        [pltpu.VMEM((features, LANES), jnp.float32), exact(pair_rows)],
    )(codebook, own)

    def decoded(name, packed):
        count = packed.shape[1]
        return call(decode_kernel, count * 0.0012, name, unit(count), [exact(count)])(packed, table)

    def step(name, ready, packed, so_far=None, whole=False):
        counts = [p.shape[1] for p in packed]
        before = [] if so_far is None else [so_far]
        operands = [*far_rows, *ready, *before, *([table] if packed else []), *packed]
        time = 0.2 + max(sum(counts) * 0.0011, sum(u.shape[1] for u in ready) * 0.0007)
        *more, best = call(
            functools.partial(step_kernel, len(ready), len(before), len(packed), whole),
            time,
            name,
            [*([unit(sum(counts))] if counts else []), row_best if whole else lane_best],
            [exact(count) for count in counts],
        )(*operands)
        return more, best

    first, table, own_unit = lax.optimization_barrier((arrived[0], table, own_unit))
    passed = exchange(first, 1, 1)
    first_unit = decoded("first", first)
    from_far, first_unit = lax.optimization_barrier((from_far, first_unit))
    far_rows = call(
        far_kernel, 0.9, "far", turned, [pltpu.VMEM(unit(row_count).shape, bf16), exact(row_count)]
    )(from_far, table)
    last, far_rows = lax.optimization_barrier((last, far_rows))
    last_passed = exchange(last, 1, 1)
    (passed_unit,), far_best = step("second", [own_unit, first_unit], [passed])
    (last_unit,), far_best = step("last", [passed_unit], [last, last_passed], far_best)
    units = [own_unit, first_unit, passed_unit, last_unit]
    rest = [last_unit]
    for latest in [codes for received in arrived[1:] for codes in (received, exchange(received, 1, 1))]:
        (more,), far_best = step("more", rest, [latest], far_best)
        rest = [more]
        units.append(more)
    _, far_best = step("far_rest", rest, [], far_best, whole=True)
    best = exchange(far_best, far, far)
    turned_scratch = [pltpu.VMEM(t.shape, t.dtype) for t in turned]
    for k in range(0, len(units), 4):
        part = call(near_kernel, 2.5, "near", row_best, turned_scratch)(own_unit, *units[k : k + 4])
        best = jnp.maximum(best, part)
    return best.reshape(row_count)


def solution(mesh):
    placed = (
        P(("parts", "group", "tile"), None),
        P(("parts", "group", "tile")),
        P(("parts", "group", "tile")),
        P(),
    )
    return jax.shard_map(
        body, mesh=mesh, in_specs=placed, out_specs=P(("parts", "group", "tile")), check_vma=False
    )
```

```python
import functools

import jax
import jax.numpy as jnp
from jax import lax
from jax.experimental import pallas as pl
from jax.experimental.pallas import tpu as pltpu
from jax.sharding import PartitionSpec as P

LANES = 128
META_ROWS = 8
VMEM_LIMIT = 8 * 1024 * 1024
BLOCK_SUBS = 16
STEP_LANES = 256
AXES = ("group", "tile")
GATHER = lax.GatherDimensionNumbers(
    offset_dims=(),
    collapsed_slice_dims=(1,),
    start_index_map=(1,),
    operand_batching_dims=(0,),
    start_indices_batching_dims=(0,),
)


def gather_lanes(table, index):
    return lax.gather(
        table, index[..., None], GATHER, slice_sizes=(1, 1), mode=lax.GatherScatterMode.PROMISE_IN_BOUNDS
    )


def integers(values):
    return values.astype(jnp.float32).astype(jnp.int32)


def read_keys(meta):
    meta = integers(meta)
    key = ((meta[3:4] * 256 + meta[2:3]) * 256 + meta[1:2]) * 256 + meta[0:1]
    return key, key - (meta[5:6] * 256 + meta[4:5])


def spread_keys(key, out_ref):
    for c in range(key.shape[1] // LANES):
        lanes = slice(c * LANES, (c + 1) * LANES)
        out_ref[lanes, :] = jnp.broadcast_to(key[:, lanes], (LANES, LANES)).T


def make_table(codebook_ref, table_ref, wide_ref, sub_dim):
    features = table_ref.shape[0]
    wide = codebook_ref[...].astype(jnp.float32).T
    for half in range(wide.shape[1] // LANES):
        lanes = slice(half * LANES, (half + 1) * LANES)
        wide_ref[...] = wide[:, lanes]
        for first in range(0, features, BLOCK_SUBS * sub_dim):
            for e in range(sub_dim):
                row = first + e * BLOCK_SUBS
                strided = wide_ref[pl.ds(first + e, BLOCK_SUBS, stride=sub_dim), :]
                table_ref[row : row + BLOCK_SUBS, lanes] = strided.astype(jnp.bfloat16)


def decode(codes, table_ref, exact_ref, out_ref, column0):
    features = table_ref.shape[0]
    subs, rows = codes.shape
    sub_dim = features // subs
    for c in range(rows // LANES):
        lanes = slice(c * LANES, (c + 1) * LANES)
        out_lanes = slice(column0 + c * LANES, column0 + (c + 1) * LANES)
        total = jnp.zeros((8, LANES), jnp.float32)
        for block in range(subs // BLOCK_SUBS):
            chosen = integers(codes[block * BLOCK_SUBS : (block + 1) * BLOCK_SUBS, lanes]).astype(jnp.int16)
            index = chosen & (LANES - 1)
            in_low = chosen < LANES
            for e in range(sub_dim):
                row = (block * sub_dim + e) * BLOCK_SUBS
                table = table_ref[row : row + BLOCK_SUBS, :]
                low, high = gather_lanes(table[:, :LANES], index), gather_lanes(table[:, LANES:], index)
                exact = jnp.where(in_low, low, high)
                exact_ref[row : row + BLOCK_SUBS, lanes] = exact
                square = exact.astype(jnp.float32)
                square = square * square
                total = total + square[:8] + square[8:]
        inverse = lax.rsqrt(jnp.sum(total, axis=0, keepdims=True) + 1e-06)
        inverse = jnp.broadcast_to(inverse, (BLOCK_SUBS, LANES))
        for row in range(0, features, BLOCK_SUBS):
            exact = exact_ref[row : row + BLOCK_SUBS, lanes].astype(jnp.float32)
            out_ref[row : row + BLOCK_SUBS, out_lanes] = (exact * inverse).astype(jnp.bfloat16)


def meta_rows(cluster, slot, group_slots, groups):
    local = slot
    for g in range(1, groups):
        local = local - jnp.where(slot >= g * group_slots, group_slots, 0)
    key = cluster * group_slots + local
    digits = [key & 255, (key >> 8) & 255, (key >> 16) & 255, key >> 24, local & 255, local >> 8]
    row = lax.broadcasted_iota(jnp.int32, (META_ROWS, key.shape[1]), 0)
    meta = jnp.zeros(row.shape, jnp.int32)
    for d, digit in enumerate(digits):
        meta = jnp.where(row == d, digit, meta)
    return meta.astype(jnp.float32).astype(jnp.bfloat16)


def pack(codes, cluster, slot, group_slots, groups):
    subs, rows = codes.shape
    meta = meta_rows(cluster.reshape(1, rows), slot.reshape(1, rows), group_slots, groups)
    return codes.astype(jnp.float32).astype(jnp.bfloat16), meta


def pack_kernel(group_slots, groups, *refs):
    sources, out_ref, buffers, sems = refs[:3], refs[3], refs[4:7], refs[7]
    copies = [
        pltpu.make_async_copy(source, buffer, sems.at[k]) for k, (source, buffer) in enumerate(zip(sources, buffers))
    ]
    for copy in copies:
        copy.start()
    for copy in copies:
        copy.wait()
    codes, meta = pack(*(buffer[...] for buffer in buffers), group_slots, groups)
    out_ref[: codes.shape[0], :] = codes
    out_ref[codes.shape[0] :, :] = meta


def join_kernel(group_slots, groups, packed_ref, codes_ref, cluster_ref, slot_ref, out_ref):
    subs, rows = codes_ref.shape
    codes, meta = pack(codes_ref[...], cluster_ref[...], slot_ref[...], group_slots, groups)
    out_ref[:, :rows] = packed_ref[...]
    out_ref[:subs, rows:] = codes
    out_ref[subs:, rows:] = meta


def unit_kernel(packed_ref, table_ref, out_ref, exact_ref, column0=0):
    features = table_ref.shape[0]
    subs, rows = packed_ref.shape[0] - META_ROWS, packed_ref.shape[1]
    decode(packed_ref[:subs, :], table_ref, exact_ref, out_ref, column0)
    out_ref[features:, column0 : column0 + rows] = packed_ref[subs:, :]


def turn(unit_ref, rows_ref, base_ref, slot_ref):
    rows, features = rows_ref.shape
    rows_ref[...] = unit_ref[:features, :rows].T
    key, base = read_keys(unit_ref[features:, :rows])
    spread_keys(base, base_ref)
    spread_keys(key - base, slot_ref)


def score(rows_ref, base_ref, slot_ref, unit_refs, best):
    features = rows_ref.shape[1]
    for unit_ref in unit_refs:
        count = unit_ref.shape[1]
        column_key, _ = read_keys(unit_ref[features:, :])
        for first in range(0, count, STEP_LANES):
            span = slice(first, min(first + STEP_LANES, count))
            scores = jnp.dot(rows_ref[...], unit_ref[:features, span], preferred_element_type=jnp.float32)
            for c in range(0, scores.shape[1], LANES):
                distance = column_key[:, first + c : first + c + LANES] - base_ref[...]
                allowed = distance.astype(jnp.uint32) < slot_ref[...].astype(jnp.uint32)
                best = jnp.maximum(best, jnp.where(allowed, scores[:, c : c + LANES], -1.0))
    return best


def nothing(shape):
    return jnp.full(shape, -1.0, jnp.float32)


def finish(best):
    rows = best.shape[0]
    pieces = [
        jnp.max(best[first : first + LANES, :].T, axis=0, keepdims=True) for first in range(0, rows, LANES)
    ]
    return jnp.concatenate(pieces, axis=1)


def own_kernel(codebook_ref, packed_ref, table_ref, unit_ref, wide_ref, exact_ref):
    subs = packed_ref.shape[0] - META_ROWS
    make_table(codebook_ref, table_ref, wide_ref, table_ref.shape[0] // subs)
    unit_kernel(packed_ref, table_ref, unit_ref, exact_ref)


def decode_kernel(*refs):
    packed_ref, table_ref, unit_ref, exact_ref = refs
    unit_kernel(packed_ref, table_ref, unit_ref, exact_ref)


def near_kernel(own_ref, *refs):
    *unit_refs, best_ref, rows_ref, key_ref, base_ref = refs
    turn(own_ref, rows_ref, key_ref, base_ref)
    best_ref[...] = finish(score(rows_ref, key_ref, base_ref, unit_refs, nothing(key_ref.shape)))


def far_kernel(packed_ref, table_ref, rows_ref, key_ref, base_ref, unit_ref, exact_ref):
    unit_kernel(packed_ref, table_ref, unit_ref, exact_ref)
    turn(unit_ref, rows_ref, key_ref, base_ref)


def step_kernel(ready, with_so_far, decoded, whole, *refs):
    refs = list(refs)
    take = lambda count: [refs.pop(0) for _ in range(count)]
    rows, unit_refs, so_far = take(3), take(ready), take(with_so_far)
    table_refs, packed_refs, out_refs = take(min(decoded, 1)), take(decoded), take(min(decoded, 1))
    best_ref, exact_refs = refs[0], refs[1:]
    best = score(*rows, unit_refs, so_far[0][...] if so_far else nothing((rows[0].shape[0], LANES)))
    best_ref[...] = finish(best) if whole else best
    column0 = 0
    for packed_ref, exact_ref in zip(packed_refs, exact_refs):
        unit_kernel(packed_ref, table_refs[0], out_refs[0], exact_ref, column0)
        column0 += packed_ref.shape[1]


VMEM = pl.BlockSpec(memory_space=pltpu.MemorySpace.VMEM)
HBM = pl.BlockSpec(memory_space=pltpu.MemorySpace.HBM)


def call(kernel, microseconds, name, out_shape, scratch=(), in_spec=VMEM):
    def run(*operands):
        return pl.pallas_call(
            kernel,
            in_specs=[in_spec] * len(operands),
            out_shape=out_shape,
            scratch_shapes=scratch,
            compiler_params=pltpu.CompilerParams(vmem_limit_bytes=VMEM_LIMIT),
            cost_estimate=pl.CostEstimate(flops=int(microseconds * 1.15e9), bytes_accessed=0, transcendentals=0),
            name=name,
        )(*operands)

    return run


def body(product_codes, member_cluster, member_slot, codebook):
    row_count, subs = product_codes.shape
    code_count, features = codebook.shape
    groups = lax.axis_size("group")
    tiles = lax.axis_size("tile")
    devices = groups * tiles
    pair_rows = 2 * row_count
    group_slots = tiles * 2 * row_count
    packed_rows = subs + META_ROWS

    def exchange(value, offset_core0, offset_core1):
        pairs = [(i, i ^ (offset_core0 if i % 2 == 0 else offset_core1)) for i in range(devices)]
        return lax.ppermute(value, AXES, pairs)

    far = (groups // 2) * tiles
    chips = [dz * tiles + dx * 2 for dz in range(groups // 2) for dx in range(tiles // 2)]
    pairs, last_chip = list(zip(chips[1:-1:2], chips[2:-1:2])), chips[-1]

    shape = jax.ShapeDtypeStruct
    bf16 = jnp.bfloat16

    def exact(count):
        return pltpu.VMEM((features, count), bf16)

    def unit(count):
        return shape((features + META_ROWS, count), bf16)

    spread = shape((row_count, LANES), jnp.int32)
    turned = (shape((row_count, features), bf16), spread, spread)
    lane_best = shape((row_count, LANES), jnp.float32)
    row_best = shape((1, row_count), jnp.float32)

    mine = (product_codes, member_cluster, member_slot)
    other_codes, other_cluster, other_slot = (exchange(value, 1, 1) for value in mine)
    packed = call(
        functools.partial(pack_kernel, group_slots, groups),
        0.3,
        "pack",
        shape((packed_rows, row_count), bf16),
        [pltpu.VMEM((subs, row_count), jnp.int32)]
        + [pltpu.VMEM((row_count,), jnp.int32)] * 2
        + [pltpu.SemaphoreType.DMA((3,))],
        in_spec=HBM,
    )(*(pltpu.with_memory_space_constraint(v, pltpu.MemorySpace.HBM) for v in (product_codes.T, *mine[1:])))
    own = call(
        functools.partial(join_kernel, group_slots, groups), 0.3, "join", shape((packed_rows, pair_rows), bf16)
    )(packed, other_codes.T, other_cluster, other_slot)
    packed, own = lax.optimization_barrier((packed, own))
    from_far = exchange(packed, far ^ 1, far ^ 1)
    arrived = [exchange(own, *pair) for pair in pairs]
    last = exchange(packed, last_chip ^ 1, last_chip ^ 1)

    table, own_unit = call(
        own_kernel,
        1.4,
        "decode_own",
        (shape((features, code_count), bf16), unit(pair_rows)),
        [pltpu.VMEM((features, LANES), jnp.float32), exact(pair_rows)],
    )(codebook, own)

    def decoded(name, packed):
        count = packed.shape[1]
        return call(decode_kernel, count * 0.0012, name, unit(count), [exact(count)])(packed, table)

    def step(name, ready, packed, so_far=None, whole=False):
        counts = [p.shape[1] for p in packed]
        before = [] if so_far is None else [so_far]
        operands = [*far_rows, *ready, *before, *([table] if packed else []), *packed]
        time = 0.2 + max(sum(counts) * 0.0011, sum(u.shape[1] for u in ready) * 0.0007)
        *more, best = call(
            functools.partial(step_kernel, len(ready), len(before), len(packed), whole),
            time,
            name,
            [*([unit(sum(counts))] if counts else []), row_best if whole else lane_best],
            [exact(count) for count in counts],
        )(*operands)
        return more, best

    first, table, own_unit = lax.optimization_barrier((arrived[0], table, own_unit))
    passed = exchange(first, 1, 1)
    first_unit = decoded("first", first)
    from_far, first_unit = lax.optimization_barrier((from_far, first_unit))
    far_rows = call(
        far_kernel, 0.9, "far", turned, [pltpu.VMEM(unit(row_count).shape, bf16), exact(row_count)]
    )(from_far, table)
    last, far_rows = lax.optimization_barrier((last, far_rows))
    last_passed = exchange(last, 1, 1)
    (passed_unit,), far_best = step("second", [own_unit, first_unit], [passed])
    (last_unit,), far_best = step("last", [passed_unit], [last, last_passed], far_best)
    units = [own_unit, first_unit, passed_unit, last_unit]
    rest = [last_unit]
    for latest in [codes for received in arrived[1:] for codes in (received, exchange(received, 1, 1))]:
        (more,), far_best = step("more", rest, [latest], far_best)
        rest = [more]
        units.append(more)
    _, far_best = step("far_rest", rest, [], far_best, whole=True)
    best = exchange(far_best, far ^ 1, far ^ 1)
    turned_scratch = [pltpu.VMEM(t.shape, t.dtype) for t in turned]
    for k in range(0, len(units), 4):
        part = call(near_kernel, 2.5, "near", row_best, turned_scratch)(own_unit, *units[k : k + 4])
        best = jnp.maximum(best, part)
    return best.reshape(row_count)


def solution(mesh):
    placed = (
        P(("parts", "group", "tile"), None),
        P(("parts", "group", "tile")),
        P(("parts", "group", "tile")),
        P(),
    )
    return jax.shard_map(
        body, mesh=mesh, in_specs=placed, out_specs=P(("parts", "group", "tile")), check_vma=False
    )
```
